512 devices in a mesh: blk: 32 (over y_hi, z, core), col: 16 (over y_lo, x).
Axes of the slice: x: 4, y: 8 (y_hi: 2, y_lo: 4; y = y_hi * 4 + y_lo), z: 8, core: 2. Of those that a mesh axis runs over, the one named last changes fastest.
Arguments:
- pair_rep: bfloat16 [512, 512, 128], P('blk', 'col'), may hold values from -6 to 6
- norm_gain: float32 [128], replicated, may hold values from 0.5 to 1.5
- norm_shift: float32 [128], replicated, may hold values from -3 to 3
- w_query: bfloat16 [128, 128], replicated, may hold values from -5 to 5
- w_key: bfloat16 [128, 128], replicated, may hold values from -5 to 5
- w_value: bfloat16 [128, 128], replicated, may hold values from -0.5 to 0.5
- w_bias: bfloat16 [128, 4], replicated, may hold values from -1.5 to 1.5
- w_gate: bfloat16 [128, 128], replicated, may hold values from -0.5 to 0.5
- gate_shift: float32 [128], replicated, may hold values from -4 to 4
- w_out: bfloat16 [128, 128], replicated, may hold values from -0.5 to 0.5
Outputs:
- update: bfloat16 [512, 512, 128], P('blk', 'col')
The draws below stay inside these ranges and needn't reach their ends.
All inputs are finite; a program needn't handle non-finite values.
Results may differ from the reference program's by a relative error of at most 0.012.
The reference program's roundings to bfloat16 on the way (of `normed`, `tri_bias`, `weights` and `hidden`) count: a program that leaves them out, or rounds other values in their place, can miss the bound.
Values may be sent and summed in bfloat16 or wider, within the bound.
A program may use at most 128 MiB of HBM per device.

```python
import jax
import jax.numpy as jnp
from jax import lax

C = 128
H = 4
HD = 32
RESIDUES = 512


def shared_weight(key):
    return jnp.clip(jax.random.normal(key, (C, C), jnp.float32), -4.0, 4.0) / C ** 0.5


def draw_pair_rep(key, part):
    key = jax.random.fold_in(key, 1)
    base_key = jax.random.fold_in(key, 0)
    field = jnp.clip(jax.random.normal(base_key, (RESIDUES, RESIDUES, C), jnp.float32), -6.0, 6.0)
    return field.astype(jnp.bfloat16)


def draw_w_query(key, part):
    key = jax.random.fold_in(key, 2)
    return shared_weight(key).astype(jnp.bfloat16)


def draw_w_key(key, part):
    key = jax.random.fold_in(key, 3)
    return shared_weight(key).astype(jnp.bfloat16)


def normal_values(stream_key, shape, deviation, reach, dtype=jnp.bfloat16):
    result = jax.random.normal(stream_key, shape, jnp.float32) * deviation
    return jnp.minimum(jnp.maximum(result, -reach), reach).astype(dtype)


def setup_inputs(seed: int = 0) -> dict:
    streams_of = jax.random.split(jax.random.key(seed), 11)
    return {
        "pair_rep": draw_pair_rep(jax.random.fold_in(streams_of[10], 71), 0),
        "norm_gain": jnp.clip(1.0 + 0.1 * jax.random.normal(streams_of[1], (C,), jnp.float32), 0.5, 1.5),
        "norm_shift": normal_values(streams_of[2], (C,), 0.5, 3.0, jnp.float32),
        "w_query": draw_w_query(jax.random.fold_in(streams_of[10], 71), 0),
        "w_key": draw_w_key(jax.random.fold_in(streams_of[10], 71), 0),
        "w_value": normal_values(streams_of[5], (C, C), C ** -0.5, 0.5),
        "w_bias": normal_values(streams_of[6], (C, H), 0.25, 1.5),
        "w_gate": normal_values(streams_of[7], (C, C), C ** -0.5, 0.5),
        "gate_shift": normal_values(streams_of[8], (C,), 1.0, 4.0, jnp.float32),
        "w_out": normal_values(streams_of[9], (C, C), C ** -0.5, 0.5),
    }


def layer_norm(pair_rep, norm_gain, norm_shift):
    centered = pair_rep.astype(jnp.float32)
    average = lax.optimization_barrier(jnp.mean(centered, axis=-1, keepdims=True))
    centered = centered - average
    variance = lax.optimization_barrier(jnp.mean(centered * centered, axis=-1, keepdims=True))
    return (centered * lax.rsqrt(variance + 1e-05) * norm_gain + norm_shift).astype(jnp.bfloat16)

def reference(pair_rep, norm_gain, norm_shift, w_query, w_key, w_value, w_bias, w_gate, gate_shift, w_out):
    normed = layer_norm(pair_rep, norm_gain, norm_shift)
    flat_normed = normed.reshape(-1, C)
    query_scale = 1.0 / HD ** 0.5
    queries = (jnp.dot(flat_normed, w_query, preferred_element_type=jnp.float32) * query_scale).astype(jnp.bfloat16)
    key_rows = jnp.dot(flat_normed, w_key, preferred_element_type=jnp.float32).astype(jnp.bfloat16)
    value_rows = jnp.dot(flat_normed, w_value, preferred_element_type=jnp.float32).astype(jnp.bfloat16)
    tri_bias = jnp.dot(flat_normed, w_bias, preferred_element_type=jnp.float32).astype(jnp.bfloat16)
    bias_turned = tri_bias.reshape(RESIDUES, RESIDUES, H).transpose(1, 2, 0).astype(jnp.float32)
    gating = jax.nn.sigmoid(jnp.dot(flat_normed, w_gate, preferred_element_type=jnp.float32) + gate_shift)

    def column(operands):
        query_col, key_col, value_col = operands
        scores = jnp.einsum('ihd,khd->ihk', query_col.astype(jnp.float32), key_col.astype(jnp.float32)) + bias_turned
        largest = lax.optimization_barrier(jnp.max(scores, axis=-1, keepdims=True))
        expo = jnp.exp(scores - largest)
        denominator = lax.optimization_barrier(jnp.sum(expo, axis=-1))
        weights = expo.astype(jnp.bfloat16)
        numerator = jnp.einsum('ihk,khd->ihd', weights.astype(jnp.float32), value_col.astype(jnp.float32))
        return numerator / denominator[..., None]
    shaped = lambda arr: arr.reshape(RESIDUES, RESIDUES, H, HD).transpose(1, 0, 2, 3)
    attended = lax.map(column, (shaped(queries), shaped(key_rows), shaped(value_rows)))
    attended = attended.transpose(1, 0, 2, 3).reshape(-1, C)
    hidden = (gating * attended).astype(jnp.bfloat16)
    update = jnp.dot(hidden, w_out, preferred_element_type=jnp.float32).astype(jnp.bfloat16)
    return update.reshape(RESIDUES, RESIDUES, C)
```

```python
import jax
import jax.numpy as jnp
from jax import lax
from jax.experimental import pallas as pl
from jax.experimental.pallas import tpu as pltpu
from jax.sharding import PartitionSpec as P

MESH = pl.DeviceIdType.MESH
ROWS, COLS, C, H, HD = 16, 32, 128, 4, 32
NZ, NX, NY, NC = 8, 4, 4, 2
JC = 4
F32, BF16 = jnp.float32, jnp.bfloat16


def device(core, z, yh, x, yl):
    return ((yh * NZ + z) * NC + core, yl * NX + x)


def remote(src, dst, send, recv, where):
    return pltpu.make_async_remote_copy(
        src_ref=src, dst_ref=dst, send_sem=send, recv_sem=recv, device_id=where, device_id_type=MESH
    )


def dot(a, b):
    return jnp.dot(a, b, preferred_element_type=F32)


def dot_nt(a, b):
    return lax.dot_general(a, b, (((1,), (1,)), ((), ())), preferred_element_type=F32)


def kernel(
    pair_ref, gain_ref, shift_ref, wq_ref, wk_ref, wv_ref, wb_ref, wg_ref, gs_ref, wo_ref,
    out_ref,
    ln_ref, norm_ref, part_ref, x_ref, tile_ref, b_ref, k_ref, vt_ref, q_ref, g_ref, upd_ref,
    z_send, z_recv, y_send, y_recv, c_send, c_recv, b_send, b_recv, x_send, x_recv, o_send, o_recv,
):
    blk, col = lax.axis_index("blk"), lax.axis_index("col")
    core, z, yh = lax.rem(blk, NC), lax.rem(blk // NC, NZ), blk // (NC * NZ)
    x, yl = lax.rem(col, NX), col // NX
    other = 1 - core
    bias_yl = yh * NC + core
    to_yh, to_core = yl // NC, lax.rem(yl, NC)
    bias_self = bias_yl == yl
    out_self = core == z // 4

    barrier = pltpu.get_barrier_semaphore()

    def greet(where):
        pl.semaphore_signal(barrier, inc=1, device_id=where, device_id_type=MESH)

    for s in range(NC * 2 * NZ):
        c_s, z_s, yh_s = s % 2, (s // 2) % NZ, s // 16
        mine = bias_self & (c_s == core) & (z_s == z) & (yh_s == yh)

        @pl.when(jnp.logical_not(mine))
        def _():
            greet(device(c_s, z_s, yh_s, x, bias_yl))

    for dz in range(1, NZ):
        greet(device(core, lax.rem(z + dz, NZ), yh, x, yl))
    greet(device(core, z, 1 - yh, x, yl))
    greet(device(other, z, yh, x, yl))
    for dx in range(1, NX):
        greet(device(core, z, yh, lax.rem(x + dx, NX), yl))
    for z_s in range(NZ):
        mine = out_self & (z_s == z)

        @pl.when(jnp.logical_not(mine))
        def _():
            greet(device(z // 4, z_s, yh, x, yl))

    wb = wb_ref[...].astype(F32)
    head = lax.broadcasted_iota(jnp.int32, (C, C), 1) // HD
    wide = jnp.zeros((C, C), F32)
    for h in range(H):
        wide = jnp.where(head == h, wb[:, h : h + 1], wide)
    wide = wide.astype(BF16)
    diagonal = (
        lax.broadcasted_iota(jnp.int32, (COLS, C), 0)
        == lax.broadcasted_iota(jnp.int32, (COLS, C), 1) % HD
    )
    gain, shift = gain_ref[...], shift_ref[...]
    for r in range(0, ROWS, 4):
        v = pair_ref[r : r + 4].reshape(4 * COLS, C).astype(F32)
        v = v - jnp.mean(v, axis=-1, keepdims=True)
        var = jnp.mean(v * v, axis=-1, keepdims=True)
        n = (v * lax.rsqrt(var + 1e-05) * gain + shift).astype(BF16)
        ln_ref[r * COLS : (r + 4) * COLS, :] = n.astype(F32)
        t = dot(n, wide).reshape(4, COLS, C)
        norm_ref[r : r + 4, :] = jnp.sum(jnp.where(diagonal[None], t, 0.0), axis=1)
    tile_ref[...] = norm_ref[...].astype(BF16)
    for j in range(COLS):
        part_ref[j // JC, j % JC] = ln_ref[pl.ds(j, ROWS, stride=COLS), :].astype(BF16)

    sends_bias = 32 - bias_self.astype(jnp.int32)
    sends_out = 8 - out_self.astype(jnp.int32)
    pl.semaphore_wait(barrier, sends_bias + sends_out + 12)

    for dz in range(NZ):
        for dy in range(NY):
            z_d, yl_d = lax.rem(z + dz, NZ), lax.rem(yl + dy, NY)
            dst = b_ref.at[x, yh, core, z]
            cp = remote(tile_ref, dst, b_send, b_recv.at[yh], device(to_core, z_d, to_yh, x, yl_d))
            if dz or dy:
                cp.start()
            else:

                @pl.when(bias_self)
                def _():
                    pltpu.make_async_copy(tile_ref, dst, b_recv.at[yh]).start()

                @pl.when(jnp.logical_not(bias_self))
                def _():
                    cp.start()

    x_ref[yh, core, z] = part_ref[z]
    for dz in range(1, NZ):
        z_d = lax.rem(z + dz, NZ)
        remote(
            part_ref.at[z_d], x_ref.at[yh, core, z], z_send, z_recv, device(core, z_d, yh, x, yl)
        ).start()
    seven = x_ref.at[0, 0, pl.ds(0, NZ - 1)]
    pltpu.make_async_copy(seven, seven, z_recv).wait()

    here = x_ref.at[yh, core]
    cp_y = remote(here, here, y_send, y_recv, device(core, z, 1 - yh, x, yl))
    cp_y.start()
    cp_c0 = remote(here, here, c_send.at[0], c_recv.at[0], device(other, z, yh, x, yl))
    cp_c0.start()

    cp_x = []
    for half in range(2):
        got = b_ref.at[x, half]
        pltpu.make_async_copy(got, got, b_recv.at[half]).wait()
        for dx in range(1, NX):
            cp = remote(
                got, got, x_send.at[half, dx - 1], x_recv.at[half, dx - 1],
                device(core, z, yh, lax.rem(x + dx, NX), yl),
            )
            cp.start()
            cp_x.append(cp)

    wk = wk_ref[...]
    wvt = wv_ref[...].astype(F32).T.astype(BF16)

    def project(half, c):
        rows = x_ref[half, c].reshape(NZ * JC * ROWS, C)
        k_ref[half, c] = dot(rows, wk).astype(BF16).reshape(NZ, JC, ROWS, C)
        for j in range(JC):
            vt_ref[j, half, c] = dot_nt(wvt, x_ref[half, c, :, j].reshape(NZ * ROWS, C)).astype(BF16)

    project(yh, core)
    cp_c0.wait_recv()
    project(yh, other)

    for s in range(NX):
        rows = x_ref[yh, :, core * 4 + s].reshape(NC * JC * ROWS, C)
        q = (dot(rows, wq_ref[...]) * (1.0 / HD**0.5)).astype(BF16)
        q_ref[s] = q.reshape(NC, JC, ROWS, C)
        g_ref[s] = jax.nn.sigmoid(dot(rows, wg_ref[...]) + gs_ref[...]).reshape(NC, JC, ROWS, C)

    cp_y.wait_recv()
    there = x_ref.at[1 - yh, core]
    cp_c1 = remote(there, there, c_send.at[1], c_recv.at[1], device(other, z, yh, x, yl))
    cp_c1.start()
    project(1 - yh, core)
    cp_c1.wait_recv()
    project(1 - yh, other)

    row_head = lax.broadcasted_iota(jnp.int32, (C, C), 0) // HD
    own_head = row_head == head
    lane_head = lax.broadcasted_iota(jnp.int32, (HD, C), 1) // HD

    for dx in range(NX):
        s = lax.rem(x + NX - dx, NX)
        if dx:
            for half in range(2):
                got = b_ref.at[s, half]
                pltpu.make_async_copy(got, got, x_recv.at[half, dx - 1]).wait()
        bias = b_ref.at[s]
        hidden = []
        for j in range(JC):
            q = q_ref[s, :, j].reshape(NC * ROWS, C)
            q = jnp.where(own_head, jnp.concatenate([q] * H, axis=0), jnp.zeros((), BF16))
            k = k_ref[:, :, :, j].reshape(512, C)
            scores = dot_nt(k, q) + bias[...].reshape(512, C).astype(F32)
            expo = jnp.exp(scores - jnp.max(scores, axis=0, keepdims=True))
            total = jnp.sum(expo, axis=0, keepdims=True)
            expo = expo.astype(BF16)
            acc = jnp.zeros((C, C), F32)
            for p in range(4):
                acc = acc + dot(vt_ref[j, p // 2, p % 2], expo[p * 128 : (p + 1) * 128])
            acc = (acc * (1.0 / total)).T
            att = jnp.zeros((HD, C), F32)
            for h in range(H):
                att = jnp.where(lane_head == h, acc[h * HD : (h + 1) * HD], att)
            hidden.append((g_ref[s, :, j].reshape(NC * ROWS, C) * att).astype(BF16))
        hidden = jnp.stack([v.reshape(NC, ROWS, C) for v in hidden], axis=1)
        update = dot(hidden.reshape(NC * JC * ROWS, C), wo_ref[...]).astype(BF16)
        upd_ref[s] = update.reshape(NC, JC, ROWS, C)
        z_d = core * 4 + s
        for c_d in range(NC):
            mine = (z_d == z) & (core == c_d)
            src, dst = upd_ref.at[s, c_d], out_ref.at[z]

            @pl.when(mine)
            def _():
                pltpu.make_async_copy(src, dst, o_recv).start()

            @pl.when(jnp.logical_not(mine))
            def _():
                remote(src, dst, o_send, o_recv, device(c_d, z_d, yh, x, yl)).start()

    pltpu.make_async_copy(out_ref, out_ref, o_recv).wait()
    cp_y.wait_send()
    cp_c0.wait_send()
    cp_c1.wait_send()
    for cp in cp_x:
        cp.wait_send()
    pltpu.make_async_copy(seven, seven, z_send).wait()
    pieces = x_ref.at[0, 0]

    @pl.when(out_self)
    def _():
        pltpu.make_async_copy(seven, seven, o_send).wait()

    @pl.when(jnp.logical_not(out_self))
    def _():
        pltpu.make_async_copy(pieces, pieces, o_send).wait()

    tiles = b_ref.at[0].reshape(32, ROWS, C)

    @pl.when(bias_self)
    def _():
        got = tiles.at[pl.ds(0, 31)]
        pltpu.make_async_copy(got, got, b_send).wait()

    @pl.when(jnp.logical_not(bias_self))
    def _():
        pltpu.make_async_copy(tiles, tiles, b_send).wait()


def per_device(
    pair_rep, norm_gain, norm_shift, w_query, w_key, w_value, w_bias, w_gate, gate_shift, w_out
):
    vmem = pl.BlockSpec(memory_space=pltpu.VMEM)
    dma = pltpu.SemaphoreType.DMA
    result = pl.pallas_call(
        kernel,
        out_shape=jax.ShapeDtypeStruct((NZ, JC, ROWS, C), BF16),
        in_specs=[vmem] * 10,
        out_specs=vmem,
        scratch_shapes=[
            pltpu.VMEM((ROWS * COLS, C), F32),
            pltpu.VMEM((ROWS, C), F32),
            pltpu.VMEM((NZ, JC, ROWS, C), BF16),
            pltpu.VMEM((2, NC, NZ, JC, ROWS, C), BF16),
            pltpu.VMEM((ROWS, C), BF16),
            pltpu.VMEM((NX, 2, NC, NZ, ROWS, C), BF16),
            pltpu.VMEM((2, NC, NZ, JC, ROWS, C), BF16),
            pltpu.VMEM((JC, 2, NC, C, NZ * ROWS), BF16),
            pltpu.VMEM((NX, NC, JC, ROWS, C), BF16),
            pltpu.VMEM((NX, NC, JC, ROWS, C), F32),
            pltpu.VMEM((NX, NC, JC, ROWS, C), BF16),
            dma, dma, dma, dma, dma((2,)), dma((2,)), dma, dma((2,)),
            dma((2, NX - 1)), dma((2, NX - 1)), dma, dma,
        ],
        compiler_params=pltpu.CompilerParams(
            collective_id=0, has_side_effects=True, vmem_limit_bytes=32 << 20
        ),
        name="triangle",
    )(
        pair_rep, norm_gain.reshape(1, C), norm_shift.reshape(1, C), w_query, w_key, w_value,
        w_bias, w_gate, gate_shift.reshape(1, C), w_out,
    )
    return result.reshape(COLS, ROWS, C).transpose(1, 0, 2)


def solution(mesh):
    placed = (P("blk", "col", None),) + (P(),) * 9
    return jax.shard_map(
        per_device, mesh=mesh, in_specs=placed, out_specs=P("blk", "col", None), check_vma=False
    )
```

```python
import jax
import jax.numpy as jnp
from jax import lax
from jax.experimental import pallas as pl
from jax.experimental.pallas import tpu as pltpu
from jax.sharding import PartitionSpec as P

MESH = pl.DeviceIdType.MESH
ROWS, COLS, C, H, HD = 16, 32, 128, 4, 32
NZ, NX, NY, NC = 8, 4, 4, 2
FAR = (4, 3, 5, 2, 6, 1, 7, 0)
NEAR = (0, 1, 7, 2, 6, 3, 5, 4)
JC = 4
F32, BF16 = jnp.float32, jnp.bfloat16


def device(core, z, yh, x, yl):
    return ((yh * NZ + z) * NC + core, yl * NX + x)


def remote(src, dst, send, recv, where):
    return pltpu.make_async_remote_copy(
        src_ref=src, dst_ref=dst, send_sem=send, recv_sem=recv, device_id=where, device_id_type=MESH
    )


def dot(a, b):
    return jnp.dot(a, b, preferred_element_type=F32)


def dot_nt(a, b):
    return lax.dot_general(a, b, (((1,), (1,)), ((), ())), preferred_element_type=F32)


def kernel(
    pair_hbm, gain_hbm, shift_hbm, wq_hbm, wk_hbm, wv_hbm, wb_hbm, wg_hbm, gs_hbm, wo_hbm,
    out_ref,
    pair_ref, gain_ref, shift_ref, wq_ref, wk_ref, wv_ref, wb_ref, wg_ref, gs_ref, wo_ref,
    ln_ref, norm_ref, part_ref, x_ref, tile_ref, b_ref, k_ref, vt_ref, q_ref, g_ref, upd_ref,
    in_sem, pair_sem,
    n_send, n_recv, c_send, c_recv, b_send, b_recv, x_send, x_recv, o_send, o_recv,
):
    loads = []
    for r in range(4):
        rows = pl.ds(r * 4, 4)
        loads.append(pltpu.make_async_copy(pair_hbm.at[rows], pair_ref.at[rows], pair_sem.at[r]))
    for i, (src, dst) in enumerate((
        (gain_hbm, gain_ref), (shift_hbm, shift_ref), (wb_hbm, wb_ref), (wk_hbm, wk_ref),
        (wv_hbm, wv_ref), (wq_hbm, wq_ref), (wg_hbm, wg_ref), (gs_hbm, gs_ref), (wo_hbm, wo_ref),
    )):
        loads.append(pltpu.make_async_copy(src, dst, in_sem.at[i]))
    for cp in loads:
        cp.start()
    blk, col = lax.axis_index("blk"), lax.axis_index("col")
    core, z, yh = lax.rem(blk, NC), lax.rem(blk // NC, NZ), blk // (NC * NZ)
    x, yl = lax.rem(col, NX), col // NX
    other = 1 - core
    bias_yl = yh * NC + core
    to_yh, to_core = yl // NC, lax.rem(yl, NC)
    bias_self = bias_yl == yl
    out_self = core == z // 4

    barrier = pltpu.get_barrier_semaphore()

    def greet(where):
        pl.semaphore_signal(barrier, inc=1, device_id=where, device_id_type=MESH)

    def unless(condition, action):
        pl.when(jnp.logical_not(condition))(action)

    for dz in FAR:
        z_s = lax.rem(z + dz, NZ)
        for yh_s in range(2):
            for c_s in range(NC):
                mine = bias_self & (c_s == core) & (yh_s == yh) & (dz == 0)
                unless(mine, lambda: greet(device(c_s, z_s, yh_s, x, bias_yl)))
        if dz:
            greet(device(core, z_s, yh, x, yl))
        greet(device(core, z_s, 1 - yh, x, yl))
        unless(out_self & (dz == 0), lambda: greet(device(z // 4, z_s, yh, x, yl)))
    for dx in range(1, NX):
        greet(device(core, z, yh, lax.rem(x + dx, NX), yl))
    greet(device(other, z, yh, x, yl))

    for cp in loads[4:7]:
        cp.wait()
    wide = jnp.concatenate([jnp.broadcast_to(wb_ref[h : h + 1].astype(F32), (HD, C)) for h in range(H)])
    wide = wide.astype(BF16)
    diagonal = (
        lax.broadcasted_iota(jnp.int32, (COLS, C), 0)
        == lax.broadcasted_iota(jnp.int32, (COLS, C), 1) % HD
    )
    gain, shift = gain_ref[...], shift_ref[...]
    for r in range(0, ROWS, 4):
        loads[r // 4].wait()
        v = pair_ref[r : r + 4].reshape(4 * COLS, C).astype(F32)
        v = v - jnp.mean(v, axis=-1, keepdims=True)
        var = jnp.mean(v * v, axis=-1, keepdims=True)
        n = (v * lax.rsqrt(var + 1e-05) * gain + shift).astype(BF16)
        ln_ref[r * COLS : (r + 4) * COLS, :] = n.astype(F32)
        t = dot_nt(n, wide).reshape(4, COLS, C)
        norm_ref[r : r + 4, :] = jnp.sum(jnp.where(diagonal[None], t, 0.0), axis=1)
    tile_ref[...] = norm_ref[...].astype(BF16)
    for j in range(COLS):
        part_ref[j // JC, j % JC] = ln_ref[pl.ds(j, ROWS, stride=COLS), :].astype(BF16)

    sends_bias = 32 - bias_self.astype(jnp.int32)
    sends_out = 8 - out_self.astype(jnp.int32)
    pl.semaphore_wait(barrier, sends_bias + sends_out + 19)

    for dz in FAR:
        z_d = lax.rem(z + dz, NZ)
        tile_dst = b_ref.at[x, yh, z, core]
        for dy in (2, 1, 3, 0):
            yl_d = lax.rem(yl + dy, NY)
            cp = remote(tile_ref, tile_dst, b_send, b_recv.at[z], device(to_core, z_d, to_yh, x, yl_d))
            if dz or dy:
                cp.start()
            else:
                pl.when(bias_self)(
                    lambda: pltpu.make_async_copy(tile_ref, tile_dst, b_recv.at[z]).start()
                )
                unless(bias_self, cp.start)
    for dz in FAR:
        z_d = lax.rem(z + dz, NZ)
        for yh_d in (1 - yh, yh):
            if dz or yh_d is not yh:
                remote(
                    part_ref.at[z_d], x_ref.at[yh, z, core], n_send, n_recv.at[yh, z],
                    device(core, z_d, yh_d, x, yl),
                ).start()
            else:
                pltpu.make_async_copy(part_ref.at[z], x_ref.at[yh, z, core], n_recv.at[yh, z]).start()

    def arrived(ref, sem):
        pltpu.make_async_copy(ref, ref, sem).wait()

    for cp in loads[7:]:
        cp.wait()
    wk = wk_ref[...]
    wvt = wv_ref[...].astype(F32).T.astype(BF16)

    for dz in NEAR:
        z_s = lax.rem(z + dz, NZ)
        got = b_ref.at[x, :, z_s]
        arrived(got, b_recv.at[z_s])
        for dx in (2, 1, 3):
            remote(
                got, got, x_send, x_recv.at[dx - 1], device(core, z, yh, lax.rem(x + dx, NX), yl)
            ).start()
    def share(half):
        for dz in NEAR:
            z_s = lax.rem(z + dz, NZ)
            here = x_ref.at[half, z_s, core]
            arrived(here, n_recv.at[half, z_s])
            remote(here, here, c_send, c_recv.at[half, z_s], device(other, z, yh, x, yl)).start()

    def project(half, four):
        for z_s in range(4):
            z_s = four * 4 + z_s
            arrived(x_ref.at[half, z_s, other], c_recv.at[half, z_s])
        part = x_ref.at[half, pl.ds(four * 4, 4)]
        rows = part[...].reshape(8 * JC * ROWS, C)
        k_ref[half, pl.ds(four * 4, 4)] = dot(rows, wk).astype(BF16).reshape(4, NC, JC, ROWS, C)
        for j in range(JC):
            vt_ref[j, half, four] = dot_nt(wvt, part[:, :, j].reshape(8 * ROWS, C)).astype(BF16)

    share(yh)
    project(yh, z // 4)
    project(yh, 1 - z // 4)

    for s in range(NX):
        rows = x_ref[yh, core * 4 + s].reshape(NC * JC * ROWS, C)
        q = (dot(rows, wq_ref[...]) * (1.0 / HD**0.5)).astype(BF16)
        q_ref[s] = q.reshape(NC, JC, ROWS, C)
        g_ref[s] = jax.nn.sigmoid(dot(rows, wg_ref[...]) + gs_ref[...]).reshape(NC, JC, ROWS, C)

    share(1 - yh)
    project(1 - yh, z // 4)
    project(1 - yh, 1 - z // 4)

    own_head = (
        lax.broadcasted_iota(jnp.int32, (C, C), 0) // HD
        == lax.broadcasted_iota(jnp.int32, (C, C), 1) // HD
    )
    lane_head = lax.broadcasted_iota(jnp.int32, (HD, C), 1) // HD

    for dx in (0, 1, 3, 2):
        s = lax.rem(x + NX - dx, NX)
        bias = b_ref.at[s]
        if dx:
            arrived(bias, x_recv.at[dx - 1])
        hidden = []
        for j in range(JC):
            q = q_ref[s, :, j].reshape(NC * ROWS, C)
            q = jnp.where(own_head, jnp.concatenate([q] * H, axis=0), jnp.zeros((), BF16))
            k = k_ref[:, :, :, j].reshape(512, C)
            scores = dot_nt(k, q) + bias[...].reshape(512, C).astype(F32)
            expo = jnp.exp(scores - jnp.max(scores, axis=0, keepdims=True))
            total = jnp.sum(expo, axis=0, keepdims=True)
            expo = expo.astype(BF16)
            acc = jnp.zeros((C, C), F32)
            for p in range(4):
                acc = acc + dot(vt_ref[j, p // 2, p % 2], expo[p * 128 : (p + 1) * 128])
            acc = (acc * (1.0 / total)).T
            att = jnp.zeros((HD, C), F32)
            for h in range(H):
                att = jnp.where(lane_head == h, acc[h * HD : (h + 1) * HD], att)
            hidden.append((g_ref[s, :, j].reshape(NC * ROWS, C) * att).astype(BF16))
        hidden = jnp.stack([v.reshape(NC, ROWS, C) for v in hidden], axis=1)
        update = dot(hidden.reshape(NC * JC * ROWS, C), wo_ref[...]).astype(BF16)
        upd_ref[s] = update.reshape(NC, JC, ROWS, C)
        z_d = core * 4 + s
        for c_d in range(NC):
            mine = (z_d == z) & (core == c_d)
            src, dst = upd_ref.at[s, c_d], out_ref.at[z]
            pl.when(mine)(lambda: pltpu.make_async_copy(src, dst, o_recv).start())
            unless(mine, remote(src, dst, o_send, o_recv, device(c_d, z_d, yh, x, yl)).start)

    arrived(out_ref, o_recv)
    pieces = x_ref.reshape(NZ * 2 * NC, JC, ROWS, C)
    tiles = b_ref.reshape(NX * 32, ROWS, C)
    arrived(pieces.at[pl.ds(0, 15)], n_send)
    arrived(pieces.at[pl.ds(0, 16)], c_send)
    arrived(b_ref.at[pl.ds(0, 3)], x_send)
    pl.when(out_self)(lambda: arrived(pieces.at[pl.ds(0, 7)], o_send))
    unless(out_self, lambda: arrived(pieces.at[pl.ds(0, 8)], o_send))
    pl.when(bias_self)(lambda: arrived(tiles.at[pl.ds(0, 31)], b_send))
    unless(bias_self, lambda: arrived(tiles.at[pl.ds(0, 32)], b_send))


def per_device(
    pair_rep, norm_gain, norm_shift, w_query, w_key, w_value, w_bias, w_gate, gate_shift, w_out
):
    dma = pltpu.SemaphoreType.DMA
    result = pl.pallas_call(
        kernel,
        out_shape=jax.ShapeDtypeStruct((NZ, JC, ROWS, C), BF16),
        in_specs=[pl.BlockSpec(memory_space=pltpu.HBM)] * 10,
        out_specs=pl.BlockSpec(memory_space=pltpu.VMEM),
        scratch_shapes=[
            pltpu.VMEM((ROWS, COLS, C), BF16),
            pltpu.VMEM((1, C), F32),
            pltpu.VMEM((1, C), F32),
            pltpu.VMEM((C, C), BF16),
            pltpu.VMEM((C, C), BF16),
            pltpu.VMEM((C, C), BF16),
            pltpu.VMEM((H, C), BF16),
            pltpu.VMEM((C, C), BF16),
            pltpu.VMEM((1, C), F32),
            pltpu.VMEM((C, C), BF16),
            pltpu.VMEM((ROWS * COLS, C), F32),
            pltpu.VMEM((ROWS, C), F32),
            pltpu.VMEM((NZ, JC, ROWS, C), BF16),
            pltpu.VMEM((2, NZ, NC, JC, ROWS, C), BF16),
            pltpu.VMEM((ROWS, C), BF16),
            pltpu.VMEM((NX, 2, NZ, NC, ROWS, C), BF16),
            pltpu.VMEM((2, NZ, NC, JC, ROWS, C), BF16),
            pltpu.VMEM((JC, 2, 2, C, 8 * ROWS), BF16),
            pltpu.VMEM((NX, NC, JC, ROWS, C), BF16),
            pltpu.VMEM((NX, NC, JC, ROWS, C), F32),
            pltpu.VMEM((NX, NC, JC, ROWS, C), BF16),
            dma((9,)), dma((4,)),
            dma, dma((2, NZ)), dma, dma((2, NZ)),
            dma, dma((NZ,)), dma, dma((NX - 1,)), dma, dma,
        ],
        compiler_params=pltpu.CompilerParams(
            collective_id=0, has_side_effects=True, vmem_limit_bytes=32 << 20
        ),
        name="triangle",
    )(*(
        pltpu.with_memory_space_constraint(v, pltpu.HBM)
        for v in (
            pair_rep, norm_gain.reshape(1, C), norm_shift.reshape(1, C), w_query, w_key, w_value,
            w_bias.T, w_gate, gate_shift.reshape(1, C), w_out,
        )
    ))
    return result.reshape(COLS, ROWS, C).transpose(1, 0, 2)


def solution(mesh):
    placed = (P("blk", "col", None),) + (P(),) * 9
    return jax.shard_map(
        per_device, mesh=mesh, in_specs=placed, out_specs=P("blk", "col", None), check_vma=False
    )
```

```python
import jax
import jax.numpy as jnp
from jax import lax
from jax.experimental import pallas as pl
from jax.experimental.pallas import tpu as pltpu
from jax.sharding import PartitionSpec as P

MESH = pl.DeviceIdType.MESH
ROWS, COLS, C, H, HD = 16, 32, 128, 4, 32
NZ, NX, NY, NC = 8, 4, 4, 2
FAR = (4, 3, 5, 2, 6, 1, 7, 0)
NEAR = (0, 1, 7, 2, 6, 3, 5, 4)
JC = 4
F32, BF16 = jnp.float32, jnp.bfloat16


def device(core, z, yh, x, yl):
    return ((yh * NZ + z) * NC + core, yl * NX + x)


def remote(src, dst, send, recv, where):
    return pltpu.make_async_remote_copy(
        src_ref=src, dst_ref=dst, send_sem=send, recv_sem=recv, device_id=where, device_id_type=MESH
    )


def dot(a, b):
    return jnp.dot(a, b, preferred_element_type=F32)


def dot_nt(a, b):
    return lax.dot_general(a, b, (((1,), (1,)), ((), ())), preferred_element_type=F32)


def kernel(
    pair_hbm, gain_hbm, shift_hbm, wq_hbm, wk_hbm, wv_hbm, wb_hbm, wg_hbm, gs_hbm, wo_hbm,
    out_ref,
    pair_ref, gain_ref, shift_ref, wq_ref, wk_ref, wv_ref, wb_ref, wg_ref, gs_ref, wo_ref,
    ln_ref, norm_ref, part_ref, x_ref, tile_ref, b_ref, k_ref, vt_ref, q_ref, g_ref, upd_ref,
    in_sem, pair_sem,
    t_send, t_recv, n_send, n_recv, y_send, y_recv, c_send, c_recv, b_send, b_recv, x_send, x_recv, o_send, o_recv,
):
    loads = []
    for r in range(4):
        rows = pl.ds(r * 4, 4)
        loads.append(pltpu.make_async_copy(pair_hbm.at[rows], pair_ref.at[rows], pair_sem.at[r]))
    for i, (src, dst) in enumerate((
        (gain_hbm, gain_ref), (shift_hbm, shift_ref), (wb_hbm, wb_ref), (wk_hbm, wk_ref),
        (wv_hbm, wv_ref), (wq_hbm, wq_ref), (wg_hbm, wg_ref), (gs_hbm, gs_ref), (wo_hbm, wo_ref),
    )):
        loads.append(pltpu.make_async_copy(src, dst, in_sem.at[i]))
    for cp in loads[:7]:
        cp.start()
    blk, col = lax.axis_index("blk"), lax.axis_index("col")
    core, z, yh = lax.rem(blk, NC), lax.rem(blk // NC, NZ), blk // (NC * NZ)
    x, yl = lax.rem(col, NX), col // NX
    other = 1 - core
    bias_yl = yh * NC + core
    to_yh, to_core = yl // NC, lax.rem(yl, NC)
    bias_self = bias_yl == yl
    out_self = core == z // 4

    barrier = pltpu.get_barrier_semaphore()

    def greet(where):
        pl.semaphore_signal(barrier, inc=1, device_id=where, device_id_type=MESH)

    def unless(condition, action):
        pl.when(jnp.logical_not(condition))(action)

    for dz in FAR:
        z_s = lax.rem(z + dz, NZ)
        if dz:
            greet(device(core, z_s, yh, x, yl))
        unless(out_self & (dz == 0), lambda: greet(device(z // 4, z_s, yh, x, yl)))
    for yh_s in range(2):
        for c_s in range(NC):
            mine = bias_self & (c_s == core) & (yh_s == yh)
            unless(mine, lambda: greet(device(c_s, z, yh_s, x, bias_yl)))
    greet(device(core, z, 1 - yh, x, yl))
    for dx in range(1, NX):
        greet(device(core, z, yh, lax.rem(x + dx, NX), yl))
    greet(device(other, z, yh, x, yl))

    for cp in loads[7:]:
        cp.start()

    for cp in loads[4:7]:
        cp.wait()
    wide = jnp.concatenate([jnp.broadcast_to(wb_ref[h : h + 1].astype(F32), (HD, C)) for h in range(H)])
    wide = wide.astype(BF16)
    diagonal = (
        lax.broadcasted_iota(jnp.int32, (COLS, C), 0)
        == lax.broadcasted_iota(jnp.int32, (COLS, C), 1) % HD
    )
    gain, shift = gain_ref[...], shift_ref[...]
    for r in range(0, ROWS, 4):
        loads[r // 4].wait()
        v = pair_ref[r : r + 4].reshape(4 * COLS, C).astype(F32)
        v = v - jnp.mean(v, axis=-1, keepdims=True)
        var = jnp.mean(v * v, axis=-1, keepdims=True)
        n = (v * lax.rsqrt(var + 1e-05) * gain + shift).astype(BF16)
        ln_ref[r * COLS : (r + 4) * COLS, :] = n.astype(F32)
        t = dot_nt(n, wide).reshape(4, COLS, C)
        norm_ref[r : r + 4, :] = jnp.sum(jnp.where(diagonal[None], t, 0.0), axis=1)
    tile_ref[...] = norm_ref[...].astype(BF16)

    for j in range(COLS):
        part_ref[j // JC, j % JC] = ln_ref[pl.ds(j, ROWS, stride=COLS), :].astype(BF16)

    sends_bias = 4 - bias_self.astype(jnp.int32)
    sends_out = 8 - out_self.astype(jnp.int32)
    pl.semaphore_wait(barrier, sends_bias + sends_out + 12)

    for dz in FAR:
        z_d = lax.rem(z + dz, NZ)
        if dz:
            remote(
                part_ref.at[z_d], x_ref.at[yh, z, core], n_send, n_recv.at[z],
                device(core, z_d, yh, x, yl),
            ).start()
        else:
            pltpu.make_async_copy(part_ref.at[z], x_ref.at[yh, z, core], n_recv.at[z]).start()

    tile_dst = b_ref.at[x, yh, z, core]
    for dy in (2, 1, 3, 0):
        yl_d = lax.rem(yl + dy, NY)
        cp = remote(tile_ref, tile_dst, t_send, t_recv, device(to_core, z, to_yh, x, yl_d))
        if dy:
            cp.start()
        else:
            pl.when(bias_self)(lambda: pltpu.make_async_copy(tile_ref, tile_dst, t_recv).start())
            unless(bias_self, cp.start)

    def arrived(ref, sem):
        pltpu.make_async_copy(ref, ref, sem).wait()

    def share(dz):
        z_s = lax.rem(z + dz, NZ)
        here = x_ref.at[yh, z_s, core]
        arrived(here, n_recv.at[z_s])
        remote(here, here, y_send, y_recv.at[z_s], device(core, z, 1 - yh, x, yl)).start()
        remote(here, here, c_send, c_recv.at[yh, z_s], device(other, z, yh, x, yl)).start()

    def spread(dz):
        z_s = lax.rem(z + dz, NZ)
        got = b_ref.at[x, :, z_s]
        if dz:
            arrived(got, b_recv.at[z_s])
        for dx in (2, 1, 3):
            remote(
                got, got, x_send, x_recv.at[dx - 1], device(core, z, yh, lax.rem(x + dx, NX), yl)
            ).start()

    def share_other():
        for dz in NEAR:
            z_s = lax.rem(z + dz, NZ)
            there = x_ref.at[1 - yh, z_s, core]
            arrived(there, y_recv.at[z_s])
            remote(there, there, c_send, c_recv.at[1 - yh, z_s], device(other, z, yh, x, yl)).start()

    share(0)
    own_z = b_ref.at[x, :, z]
    arrived(own_z, t_recv)
    for dz in FAR[:-1]:
        remote(
            own_z, own_z, b_send, b_recv.at[z], device(core, lax.rem(z + dz, NZ), yh, x, yl)
        ).start()
    spread(0)
    for dz in NEAR[1:]:
        share(dz)
    for dz in NEAR[1:]:
        spread(dz)

    for cp in loads[7:]:
        cp.wait()
    wk = wk_ref[...]
    wvt = wv_ref[...].astype(F32).T.astype(BF16)

    def project(half, four):
        for z_s in range(4):
            z_s = four * 4 + z_s
            arrived(x_ref.at[half, z_s, other], c_recv.at[half, z_s])
        part = x_ref.at[half, pl.ds(four * 4, 4)]
        rows = part[...].reshape(8 * JC * ROWS, C)
        k_ref[half, pl.ds(four * 4, 4)] = dot(rows, wk).astype(BF16).reshape(4, NC, JC, ROWS, C)
        for j in range(JC):
            vt_ref[j, half, four] = dot_nt(wvt, part[:, :, j].reshape(8 * ROWS, C)).astype(BF16)

    project(yh, z // 4)
    project(yh, 1 - z // 4)

    for s in range(NX):
        rows = x_ref[yh, core * 4 + s].reshape(NC * JC * ROWS, C)
        q = (dot(rows, wq_ref[...]) * (1.0 / HD**0.5)).astype(BF16)
        q_ref[s] = q.reshape(NC, JC, ROWS, C)
        g_ref[s] = jax.nn.sigmoid(dot(rows, wg_ref[...]) + gs_ref[...]).reshape(NC, JC, ROWS, C)

    share_other()
    project(1 - yh, z // 4)
    project(1 - yh, 1 - z // 4)

    own_head = (
        lax.broadcasted_iota(jnp.int32, (C, C), 0) // HD
        == lax.broadcasted_iota(jnp.int32, (C, C), 1) // HD
    )
    lane_head = lax.broadcasted_iota(jnp.int32, (HD, C), 1) // HD

    for dx in (0, 1, 3, 2):
        s = lax.rem(x + NX - dx, NX)
        bias = b_ref.at[s]
        if dx:
            arrived(bias, x_recv.at[dx - 1])
        hidden = []
        for j in range(JC):
            q = q_ref[s, :, j].reshape(NC * ROWS, C)
            q = jnp.where(own_head, jnp.concatenate([q] * H, axis=0), jnp.zeros((), BF16))
            k = k_ref[:, :, :, j].reshape(512, C)
            scores = dot_nt(k, q) + bias[...].reshape(512, C).astype(F32)
            expo = jnp.exp(scores - jnp.max(scores, axis=0, keepdims=True))
            total = jnp.sum(expo, axis=0, keepdims=True)
            expo = expo.astype(BF16)
            acc = jnp.zeros((C, C), F32)
            for p in range(4):
                acc = acc + dot(vt_ref[j, p // 2, p % 2], expo[p * 128 : (p + 1) * 128])
            acc = (acc * (1.0 / total)).T
            att = jnp.zeros((HD, C), F32)
            for h in range(H):
                att = jnp.where(lane_head == h, acc[h * HD : (h + 1) * HD], att)
            hidden.append((g_ref[s, :, j].reshape(NC * ROWS, C) * att).astype(BF16))
        hidden = jnp.stack([v.reshape(NC, ROWS, C) for v in hidden], axis=1)
        update = dot(hidden.reshape(NC * JC * ROWS, C), wo_ref[...]).astype(BF16)
        upd_ref[s] = update.reshape(NC, JC, ROWS, C)
        z_d = core * 4 + s
        for c_d in range(NC):
            mine = (z_d == z) & (core == c_d)
            src, dst = upd_ref.at[s, c_d], out_ref.at[z]
            pl.when(mine)(lambda: pltpu.make_async_copy(src, dst, o_recv).start())
            unless(mine, remote(src, dst, o_send, o_recv, device(c_d, z_d, yh, x, yl)).start)

    arrived(out_ref, o_recv)
    pieces = x_ref.reshape(NZ * 2 * NC, JC, ROWS, C)
    tiles = b_ref.reshape(NX * 32, ROWS, C)
    arrived(pieces.at[pl.ds(0, 7)], n_send)
    arrived(pieces.at[pl.ds(0, 8)], y_send)
    arrived(pieces.at[pl.ds(0, 16)], c_send)
    arrived(b_ref.at[pl.ds(0, 3)], x_send)
    pl.when(out_self)(lambda: arrived(pieces.at[pl.ds(0, 7)], o_send))
    unless(out_self, lambda: arrived(pieces.at[pl.ds(0, 8)], o_send))
    arrived(tiles.at[pl.ds(0, 28)], b_send)
    pl.when(bias_self)(lambda: arrived(tiles.at[pl.ds(0, 3)], t_send))
    unless(bias_self, lambda: arrived(tiles.at[pl.ds(0, 4)], t_send))


def per_device(
    pair_rep, norm_gain, norm_shift, w_query, w_key, w_value, w_bias, w_gate, gate_shift, w_out
):
    dma = pltpu.SemaphoreType.DMA
    result = pl.pallas_call(
        kernel,
        out_shape=jax.ShapeDtypeStruct((NZ, JC, ROWS, C), BF16),
        in_specs=[pl.BlockSpec(memory_space=pltpu.HBM)] * 10,
        out_specs=pl.BlockSpec(memory_space=pltpu.VMEM),
        scratch_shapes=[
            pltpu.VMEM((ROWS, COLS, C), BF16),
            pltpu.VMEM((1, C), F32),
            pltpu.VMEM((1, C), F32),
            pltpu.VMEM((C, C), BF16),
            pltpu.VMEM((C, C), BF16),
            pltpu.VMEM((C, C), BF16),
            pltpu.VMEM((H, C), BF16),
            pltpu.VMEM((C, C), BF16),
            pltpu.VMEM((1, C), F32),
            pltpu.VMEM((C, C), BF16),
            pltpu.VMEM((ROWS * COLS, C), F32),
            pltpu.VMEM((ROWS, C), F32),
            pltpu.VMEM((NZ, JC, ROWS, C), BF16),
            pltpu.VMEM((2, NZ, NC, JC, ROWS, C), BF16),
            pltpu.VMEM((ROWS, C), BF16),
            pltpu.VMEM((NX, 2, NZ, NC, ROWS, C), BF16),
            pltpu.VMEM((2, NZ, NC, JC, ROWS, C), BF16),
            pltpu.VMEM((JC, 2, 2, C, 8 * ROWS), BF16),
            pltpu.VMEM((NX, NC, JC, ROWS, C), BF16),
            pltpu.VMEM((NX, NC, JC, ROWS, C), F32),
            pltpu.VMEM((NX, NC, JC, ROWS, C), BF16),
            dma((9,)), dma((4,)),
            dma, dma, dma, dma((NZ,)), dma, dma((NZ,)), dma, dma((2, NZ)),
            dma, dma((NZ,)), dma, dma((NX - 1,)), dma, dma,
        ],
        compiler_params=pltpu.CompilerParams(
            collective_id=0, has_side_effects=True, vmem_limit_bytes=32 << 20
        ),
        name="triangle",
    )(*(
        pltpu.with_memory_space_constraint(v, pltpu.HBM)
        for v in (
            pair_rep, norm_gain.reshape(1, C), norm_shift.reshape(1, C), w_query, w_key, w_value,
            w_bias.T, w_gate, gate_shift.reshape(1, C), w_out,
        )
    ))
    return result.reshape(COLS, ROWS, C).transpose(1, 0, 2)


def solution(mesh):
    placed = (P("blk", "col", None),) + (P(),) * 9
    return jax.shard_map(
        per_device, mesh=mesh, in_specs=placed, out_specs=P("blk", "col", None), check_vma=False
    )
```

```python
import jax
import jax.numpy as jnp
from jax import lax
from jax.experimental import pallas as pl
from jax.experimental.pallas import tpu as pltpu
from jax.sharding import PartitionSpec as P

MESH = pl.DeviceIdType.MESH
ROWS, COLS, C, H, HD = 16, 32, 128, 4, 32
NZ, NX, NY, NC = 8, 4, 4, 2
FAR = (4, 3, 5, 2, 6, 1, 7, 0)
NEAR = (0, 1, 7, 2, 6, 3, 5, 4)
JC = 4
F32, BF16 = jnp.float32, jnp.bfloat16


def device(core, z, yh, x, yl):
    return ((yh * NZ + z) * NC + core, yl * NX + x)


def remote(src, dst, send, recv, where):
    return pltpu.make_async_remote_copy(
        src_ref=src, dst_ref=dst, send_sem=send, recv_sem=recv, device_id=where, device_id_type=MESH
    )


def dot(a, b):
    return jnp.dot(a, b, preferred_element_type=F32)


def dot_nt(a, b):
    return lax.dot_general(a, b, (((1,), (1,)), ((), ())), preferred_element_type=F32)


def kernel(
    pair_hbm, gain_hbm, shift_hbm, wq_hbm, wk_hbm, wv_hbm, wb_hbm, wg_hbm, gs_hbm, wo_hbm,
    out_ref,
    pair_ref, gain_ref, shift_ref, wq_ref, wk_ref, wv_ref, wb_ref, wg_ref, gs_ref, wo_ref,
    ln_ref, norm_ref, part_ref, x_ref, tile_ref, b_ref, k_ref, vt_ref, q_ref, g_ref, upd_ref,
    in_sem, pair_sem,
    t_send, t_recv, n_send, n_recv, y_send, y_recv, c_send, c_recv, b_send, b_recv, x_send, x_recv, o_send, o_recv,
):
    loads = []
    for r in range(4):
        rows = pl.ds(r * 4, 4)
        loads.append(pltpu.make_async_copy(pair_hbm.at[rows], pair_ref.at[rows], pair_sem.at[r]))
    for i, (src, dst) in enumerate((
        (gain_hbm, gain_ref), (shift_hbm, shift_ref), (wb_hbm, wb_ref), (wk_hbm, wk_ref),
        (wv_hbm, wv_ref), (wq_hbm, wq_ref), (wg_hbm, wg_ref), (gs_hbm, gs_ref), (wo_hbm, wo_ref),
    )):
        loads.append(pltpu.make_async_copy(src, dst, in_sem.at[i]))
    for cp in loads[:7]:
        cp.start()
    blk, col = lax.axis_index("blk"), lax.axis_index("col")
    core, z, yh = lax.rem(blk, NC), lax.rem(blk // NC, NZ), blk // (NC * NZ)
    x, yl = lax.rem(col, NX), col // NX
    other = 1 - core
    bias_yl = yh * NC + core
    to_yh, to_core = yl // NC, lax.rem(yl, NC)
    bias_self = bias_yl == yl
    out_self = core == z // 4

    barrier = pltpu.get_barrier_semaphore()

    def greet(where):
        pl.semaphore_signal(barrier, inc=1, device_id=where, device_id_type=MESH)

    def unless(condition, action):
        pl.when(jnp.logical_not(condition))(action)

    for dz in FAR:
        z_s = lax.rem(z + dz, NZ)
        if dz:
            greet(device(core, z_s, yh, x, yl))
        unless(out_self & (dz == 0), lambda: greet(device(z // 4, z_s, yh, x, yl)))
    for yh_s in range(2):
        for c_s in range(NC):
            mine = bias_self & (c_s == core) & (yh_s == yh)
            unless(mine, lambda: greet(device(c_s, z, yh_s, x, bias_yl)))
    greet(device(core, z, 1 - yh, x, yl))
    for dx in range(1, NX):
        greet(device(core, z, yh, lax.rem(x + dx, NX), yl))
    greet(device(other, z, yh, x, yl))


    for cp in loads[4:7]:
        cp.wait()
    wide = jnp.concatenate([jnp.broadcast_to(wb_ref[h : h + 1].astype(F32), (HD, C)) for h in range(H)])
    wide = wide.astype(BF16)
    diagonal = (
        lax.broadcasted_iota(jnp.int32, (COLS, C), 0)
        == lax.broadcasted_iota(jnp.int32, (COLS, C), 1) % HD
    )
    gain, shift = gain_ref[...], shift_ref[...]
    for r in range(0, ROWS, 16):
        for cp in loads[r // 4 : (r + 16) // 4]:
            cp.wait()
        v = pair_ref[r : r + 16].reshape(16 * COLS, C).astype(F32)
        v = v - jnp.mean(v, axis=-1, keepdims=True)
        var = jnp.mean(v * v, axis=-1, keepdims=True)
        n = (v * lax.rsqrt(var + 1e-05) * gain + shift).astype(BF16)
        ln_ref[r * COLS : (r + 16) * COLS, :] = n.astype(F32)
        t = dot_nt(n, wide).reshape(16, COLS, C)
        norm_ref[r : r + 16, :] = jnp.sum(jnp.where(diagonal[None], t, 0.0), axis=1)
    tile_ref[...] = norm_ref[...].astype(BF16)

    for j in range(COLS):
        part_ref[j // JC, j % JC] = ln_ref[pl.ds(j, ROWS, stride=COLS), :].astype(BF16)

    sends_bias = 4 - bias_self.astype(jnp.int32)
    sends_out = 8 - out_self.astype(jnp.int32)
    pl.semaphore_wait(barrier, sends_bias + sends_out + 12)

    for dz in FAR:
        z_d = lax.rem(z + dz, NZ)
        if dz:
            remote(
                part_ref.at[z_d], x_ref.at[yh, z, core], n_send, n_recv.at[z],
                device(core, z_d, yh, x, yl),
            ).start()
        else:
            pltpu.make_async_copy(part_ref.at[z], x_ref.at[yh, z, core], n_recv.at[z]).start()

    for cp in loads[7:]:
        cp.start()

    tile_dst = b_ref.at[x, yh, z, core]
    for dy in (2, 1, 3, 0):
        yl_d = lax.rem(yl + dy, NY)
        cp = remote(tile_ref, tile_dst, t_send, t_recv, device(to_core, z, to_yh, x, yl_d))
        if dy:
            cp.start()
        else:
            pl.when(bias_self)(lambda: pltpu.make_async_copy(tile_ref, tile_dst, t_recv).start())
            unless(bias_self, cp.start)

    def arrived(ref, sem):
        pltpu.make_async_copy(ref, ref, sem).wait()

    def share(dz):
        z_s = lax.rem(z + dz, NZ)
        here = x_ref.at[yh, z_s, core]
        arrived(here, n_recv.at[z_s])
        remote(here, here, y_send, y_recv.at[z_s], device(core, z, 1 - yh, x, yl)).start()
        remote(here, here, c_send, c_recv.at[yh, z_s], device(other, z, yh, x, yl)).start()

    def spread(dz):
        z_s = lax.rem(z + dz, NZ)
        got = b_ref.at[x, :, z_s]
        if dz:
            arrived(got, b_recv.at[z_s])
        for dx in (2, 1, 3):
            remote(
                got, got, x_send, x_recv.at[dx - 1], device(core, z, yh, lax.rem(x + dx, NX), yl)
            ).start()

    def share_other():
        for dz in NEAR:
            z_s = lax.rem(z + dz, NZ)
            there = x_ref.at[1 - yh, z_s, core]
            arrived(there, y_recv.at[z_s])
            remote(there, there, c_send, c_recv.at[1 - yh, z_s], device(other, z, yh, x, yl)).start()

    share(0)
    own_z = b_ref.at[x, :, z]
    arrived(own_z, t_recv)
    for dz in FAR[:-1]:
        remote(
            own_z, own_z, b_send, b_recv.at[z], device(core, lax.rem(z + dz, NZ), yh, x, yl)
        ).start()
    spread(0)
    for dz in NEAR[1:]:
        share(dz)
    for dz in NEAR[1:]:
        spread(dz)

    for cp in loads[7:]:
        cp.wait()
    wk = wk_ref[...]
    wvt = wv_ref[...].astype(F32).T.astype(BF16)

    def project(half, four):
        for z_s in range(4):
            z_s = four * 4 + z_s
            arrived(x_ref.at[half, z_s, other], c_recv.at[half, z_s])
        part = x_ref.at[half, pl.ds(four * 4, 4)]
        rows = part[...].reshape(8 * JC * ROWS, C)
        k_ref[half, pl.ds(four * 4, 4)] = dot(rows, wk).astype(BF16).reshape(4, NC, JC, ROWS, C)
        for j in range(JC):
            vt_ref[j, half, four] = dot_nt(wvt, part[:, :, j].reshape(8 * ROWS, C)).astype(BF16)

    project(yh, z // 4)
    project(yh, 1 - z // 4)

    for s in range(NX):
        rows = x_ref[yh, core * 4 + s].reshape(NC * JC * ROWS, C)
        q = (dot(rows, wq_ref[...]) * (1.0 / HD**0.5)).astype(BF16)
        q_ref[s] = q.reshape(NC, JC, ROWS, C)
        g_ref[s] = jax.nn.sigmoid(dot(rows, wg_ref[...]) + gs_ref[...]).reshape(NC, JC, ROWS, C)

    share_other()
    project(1 - yh, z // 4)
    project(1 - yh, 1 - z // 4)

    own_head = (
        lax.broadcasted_iota(jnp.int32, (C, C), 0) // HD
        == lax.broadcasted_iota(jnp.int32, (C, C), 1) // HD
    )
    lane_head = lax.broadcasted_iota(jnp.int32, (HD, C), 1) // HD

    def way(dx):
        steps = lax.rem(core * 4 + lax.rem(x + NX - dx, NX) - z + NZ, NZ)
        return jnp.minimum(steps, NZ - steps)

    one, two, three = way(1), way(2), way(3)
    last = jnp.where((one <= two) & (one <= three), 1, jnp.where(three <= two, 3, 2))
    turns = (0, jnp.where(last == 1, 3, 1), jnp.where(last == 2, 3, 2), last)
    for turn, dx in enumerate(turns):
        s = lax.rem(x + NX - dx, NX)
        bias = b_ref.at[s]
        if turn:
            arrived(bias, x_recv.at[dx - 1])
        hidden = []
        for j in range(JC):
            q = q_ref[s, :, j].reshape(NC * ROWS, C)
            q = jnp.where(own_head, jnp.concatenate([q] * H, axis=0), jnp.zeros((), BF16))
            k = k_ref[:, :, :, j].reshape(512, C)
            scores = dot_nt(k, q) + bias[...].reshape(512, C).astype(F32)
            expo = jnp.exp(scores - jnp.max(scores, axis=0, keepdims=True))
            total = jnp.sum(expo, axis=0, keepdims=True)
            expo = expo.astype(BF16)
            acc = jnp.zeros((C, C), F32)
            for p in range(4):
                acc = acc + dot(vt_ref[j, p // 2, p % 2], expo[p * 128 : (p + 1) * 128])
            acc = (acc * (1.0 / total)).T
            att = jnp.zeros((HD, C), F32)
            for h in range(H):
                att = jnp.where(lane_head == h, acc[h * HD : (h + 1) * HD], att)
            hidden.append((g_ref[s, :, j].reshape(NC * ROWS, C) * att).astype(BF16))
        hidden = jnp.stack([v.reshape(NC, ROWS, C) for v in hidden], axis=1)
        update = dot(hidden.reshape(NC * JC * ROWS, C), wo_ref[...]).astype(BF16)
        upd_ref[s] = update.reshape(NC, JC, ROWS, C)
        z_d = core * 4 + s
        for c_d in range(NC):
            mine = (z_d == z) & (core == c_d)
            src, dst = upd_ref.at[s, c_d], out_ref.at[z]
            pl.when(mine)(lambda: pltpu.make_async_copy(src, dst, o_recv).start())
            unless(mine, remote(src, dst, o_send, o_recv, device(c_d, z_d, yh, x, yl)).start)

    arrived(out_ref, o_recv)
    pieces = x_ref.reshape(NZ * 2 * NC, JC, ROWS, C)
    tiles = b_ref.reshape(NX * 32, ROWS, C)
    arrived(pieces.at[pl.ds(0, 7)], n_send)
    arrived(pieces.at[pl.ds(0, 8)], y_send)
    arrived(pieces.at[pl.ds(0, 16)], c_send)
    arrived(b_ref.at[pl.ds(0, 3)], x_send)
    pl.when(out_self)(lambda: arrived(pieces.at[pl.ds(0, 7)], o_send))
    unless(out_self, lambda: arrived(pieces.at[pl.ds(0, 8)], o_send))
    arrived(tiles.at[pl.ds(0, 28)], b_send)
    pl.when(bias_self)(lambda: arrived(tiles.at[pl.ds(0, 3)], t_send))
    unless(bias_self, lambda: arrived(tiles.at[pl.ds(0, 4)], t_send))


def per_device(
    pair_rep, norm_gain, norm_shift, w_query, w_key, w_value, w_bias, w_gate, gate_shift, w_out
):
    dma = pltpu.SemaphoreType.DMA
    result = pl.pallas_call(
        kernel,
        out_shape=jax.ShapeDtypeStruct((NZ, JC, ROWS, C), BF16),
        in_specs=[pl.BlockSpec(memory_space=pltpu.HBM)] * 10,
        out_specs=pl.BlockSpec(memory_space=pltpu.VMEM),
        scratch_shapes=[
            pltpu.VMEM((ROWS, COLS, C), BF16),
            pltpu.VMEM((1, C), F32),
            pltpu.VMEM((1, C), F32),
            pltpu.VMEM((C, C), BF16),
            pltpu.VMEM((C, C), BF16),
            pltpu.VMEM((C, C), BF16),
            pltpu.VMEM((H, C), BF16),
            pltpu.VMEM((C, C), BF16),
            pltpu.VMEM((1, C), F32),
            pltpu.VMEM((C, C), BF16),
            pltpu.VMEM((ROWS * COLS, C), F32),
            pltpu.VMEM((ROWS, C), F32),
            pltpu.VMEM((NZ, JC, ROWS, C), BF16),
            pltpu.VMEM((2, NZ, NC, JC, ROWS, C), BF16),
            pltpu.VMEM((ROWS, C), BF16),
            pltpu.VMEM((NX, 2, NZ, NC, ROWS, C), BF16),
            pltpu.VMEM((2, NZ, NC, JC, ROWS, C), BF16),
            pltpu.VMEM((JC, 2, 2, C, 8 * ROWS), BF16),
            pltpu.VMEM((NX, NC, JC, ROWS, C), BF16),
            pltpu.VMEM((NX, NC, JC, ROWS, C), F32),
            pltpu.VMEM((NX, NC, JC, ROWS, C), BF16),
            dma((9,)), dma((4,)),
            dma, dma, dma, dma((NZ,)), dma, dma((NZ,)), dma, dma((2, NZ)),
            dma, dma((NZ,)), dma, dma((NX - 1,)), dma, dma,
        ],
        compiler_params=pltpu.CompilerParams(
            collective_id=0, has_side_effects=True, vmem_limit_bytes=32 << 20
        ),
        name="triangle",
    )(*(
        pltpu.with_memory_space_constraint(v, pltpu.HBM)
        for v in (
            pair_rep, norm_gain.reshape(1, C), norm_shift.reshape(1, C), w_query, w_key, w_value,
            w_bias.T, w_gate, gate_shift.reshape(1, C), w_out,
        )
    ))
    return result.reshape(COLS, ROWS, C).transpose(1, 0, 2)


def solution(mesh):
    placed = (P("blk", "col", None),) + (P(),) * 9
    return jax.shard_map(
        per_device, mesh=mesh, in_specs=placed, out_specs=P("blk", "col", None), check_vma=False
    )
```

```python
import jax
import jax.numpy as jnp
from jax import lax
from jax.experimental import pallas as pl
from jax.experimental.pallas import tpu as pltpu
from jax.sharding import PartitionSpec as P

MESH = pl.DeviceIdType.MESH
ROWS, COLS, C, H, HD = 16, 32, 128, 4, 32
NZ, NX, NY, NC = 8, 4, 4, 2
FAR = (4, 3, 5, 2, 6, 1, 7, 0)
NEAR = (0, 1, 7, 2, 6, 3, 5, 4)
JC = 4
F32, BF16 = jnp.float32, jnp.bfloat16


def device(core, z, yh, x, yl):
    return ((yh * NZ + z) * NC + core, yl * NX + x)


def remote(src, dst, send, recv, where):
    return pltpu.make_async_remote_copy(
        src_ref=src, dst_ref=dst, send_sem=send, recv_sem=recv, device_id=where, device_id_type=MESH
    )


def dot(a, b):
    return jnp.dot(a, b, preferred_element_type=F32)


def dot_nt(a, b):
    return lax.dot_general(a, b, (((1,), (1,)), ((), ())), preferred_element_type=F32)


def kernel(
    pair_hbm, gain_hbm, shift_hbm, wq_hbm, wk_hbm, wv_hbm, wb_hbm, wg_hbm, gs_hbm, wo_hbm,
    out_ref,
    pair_ref, gain_ref, shift_ref, wq_ref, wk_ref, wv_ref, wb_ref, wg_ref, gs_ref, wo_ref,
    ln_ref, norm_ref, part_ref, x_ref, tile_ref, b_ref, k_ref, vt_ref, q_ref, g_ref, upd_ref,
    in_sem, pair_sem,
    t_send, t_recv, n_send, n_recv, y_send, y_recv, c_send, h_recv, c_recv, b_send, b_recv, x_send, x_recv, o_send, o_recv,
):
    loads = []
    for r in range(4):
        rows = pl.ds(r * 4, 4)
        loads.append(pltpu.make_async_copy(pair_hbm.at[rows], pair_ref.at[rows], pair_sem.at[r]))
    for i, (src, dst) in enumerate((
        (gain_hbm, gain_ref), (shift_hbm, shift_ref), (wb_hbm, wb_ref), (wk_hbm, wk_ref),
        (wv_hbm, wv_ref), (wq_hbm, wq_ref), (wg_hbm, wg_ref), (gs_hbm, gs_ref), (wo_hbm, wo_ref),
    )):
        loads.append(pltpu.make_async_copy(src, dst, in_sem.at[i]))
    for cp in loads[:7]:
        cp.start()
    blk, col = lax.axis_index("blk"), lax.axis_index("col")
    core, z, yh = lax.rem(blk, NC), lax.rem(blk // NC, NZ), blk // (NC * NZ)
    x, yl = lax.rem(col, NX), col // NX
    other = 1 - core
    bias_yl = yh * NC + core
    to_yh, to_core = yl // NC, lax.rem(yl, NC)
    bias_self = bias_yl == yl
    out_self = core == z // 4

    barrier = pltpu.get_barrier_semaphore()

    def greet(where):
        pl.semaphore_signal(barrier, inc=1, device_id=where, device_id_type=MESH)

    def unless(condition, action):
        pl.when(jnp.logical_not(condition))(action)

    for dz in FAR:
        z_s = lax.rem(z + dz, NZ)
        if dz:
            greet(device(core, z_s, yh, x, yl))
        unless(out_self & (dz == 0), lambda: greet(device(z // 4, z_s, yh, x, yl)))
    for yh_s in range(2):
        for c_s in range(NC):
            mine = bias_self & (c_s == core) & (yh_s == yh)
            unless(mine, lambda: greet(device(c_s, z, yh_s, x, bias_yl)))
    greet(device(core, z, 1 - yh, x, yl))
    for dx in range(1, NX):
        greet(device(core, z, yh, lax.rem(x + dx, NX), yl))
    greet(device(other, z, yh, x, yl))


    for cp in loads[4:7]:
        cp.wait()
    wide = jnp.concatenate([jnp.broadcast_to(wb_ref[h : h + 1].astype(F32), (HD, C)) for h in range(H)])
    wide = wide.astype(BF16)
    diagonal = (
        lax.broadcasted_iota(jnp.int32, (COLS, C), 0)
        == lax.broadcasted_iota(jnp.int32, (COLS, C), 1) % HD
    )
    gain, shift = gain_ref[...], shift_ref[...]
    for r in range(0, ROWS, 16):
        for cp in loads[r // 4 : (r + 16) // 4]:
            cp.wait()
        v = pair_ref[r : r + 16].reshape(16 * COLS, C).astype(F32)
        v = v - jnp.mean(v, axis=-1, keepdims=True)
        var = jnp.mean(v * v, axis=-1, keepdims=True)
        n = (v * lax.rsqrt(var + 1e-05) * gain + shift).astype(BF16)
        ln_ref[r * COLS : (r + 16) * COLS, :] = n.astype(F32)
        t = dot_nt(n, wide).reshape(16, COLS, C)
        norm_ref[r : r + 16, :] = jnp.sum(jnp.where(diagonal[None], t, 0.0), axis=1)
    tile_ref[...] = norm_ref[...].astype(BF16)

    for j in range(COLS):
        part_ref[j // JC, j % JC] = ln_ref[pl.ds(j, ROWS, stride=COLS), :].astype(BF16)

    sends_bias = 4 - bias_self.astype(jnp.int32)
    sends_out = 8 - out_self.astype(jnp.int32)
    pl.semaphore_wait(barrier, sends_bias + sends_out + 12)

    for dz in FAR:
        z_d = lax.rem(z + dz, NZ)
        if dz:
            remote(
                part_ref.at[z_d], x_ref.at[yh, z, core], n_send, n_recv.at[z],
                device(core, z_d, yh, x, yl),
            ).start()
        else:
            pltpu.make_async_copy(part_ref.at[z], x_ref.at[yh, z, core], n_recv.at[z]).start()

    for cp in loads[7:]:
        cp.start()

    tile_dst = b_ref.at[x, yh, z, core]
    for dy in (2, 1, 3, 0):
        yl_d = lax.rem(yl + dy, NY)
        cp = remote(tile_ref, tile_dst, t_send, t_recv, device(to_core, z, to_yh, x, yl_d))
        if dy:
            cp.start()
        else:
            pl.when(bias_self)(lambda: pltpu.make_async_copy(tile_ref, tile_dst, t_recv).start())
            unless(bias_self, cp.start)

    def arrived(ref, sem):
        pltpu.make_async_copy(ref, ref, sem).wait()

    def share(dz):
        z_s = lax.rem(z + dz, NZ)
        here = x_ref.at[yh, z_s, core]
        arrived(here, n_recv.at[z_s])
        remote(here, here, y_send, y_recv.at[z_s], device(core, z, 1 - yh, x, yl)).start()

    def spread(dz):
        z_s = lax.rem(z + dz, NZ)
        got = b_ref.at[x, :, z_s]
        if dz:
            arrived(got, b_recv.at[z_s])
        for dx in (2, 1, 3):
            remote(
                got, got, x_send, x_recv.at[dx - 1], device(core, z, yh, lax.rem(x + dx, NX), yl)
            ).start()

    def share_other():
        for dz in NEAR:
            z_s = lax.rem(z + dz, NZ)
            there = x_ref.at[1 - yh, z_s, core]
            arrived(there, y_recv.at[z_s])
            remote(there, there, c_send, c_recv.at[z_s], device(other, z, yh, x, yl)).start()

    share(0)
    own_z = b_ref.at[x, :, z]
    arrived(own_z, t_recv)
    for dz in FAR[:-1]:
        remote(
            own_z, own_z, b_send, b_recv.at[z], device(core, lax.rem(z + dz, NZ), yh, x, yl)
        ).start()
    spread(0)
    for dz in NEAR[1:]:
        share(dz)
    mine = x_ref.at[yh, :, core]
    remote(mine, mine, c_send, h_recv, device(other, z, yh, x, yl)).start()
    for dz in NEAR[1:]:
        spread(dz)

    for cp in loads[7:]:
        cp.wait()
    wk = wk_ref[...]
    wvt = wv_ref[...].astype(F32).T.astype(BF16)

    def project(half, four):
        if half is not yh:
            for z_s in range(4):
                z_s = four * 4 + z_s
                arrived(x_ref.at[half, z_s, other], c_recv.at[z_s])
        part = x_ref.at[half, pl.ds(four * 4, 4)]
        rows = part[...].reshape(8 * JC * ROWS, C)
        k_ref[half, pl.ds(four * 4, 4)] = dot(rows, wk).astype(BF16).reshape(4, NC, JC, ROWS, C)
        for j in range(JC):
            vt_ref[j, half, four] = dot_nt(wvt, part[:, :, j].reshape(8 * ROWS, C)).astype(BF16)

    arrived(x_ref.at[yh, :, other], h_recv)
    project(yh, z // 4)
    project(yh, 1 - z // 4)
    share_other()

    for s in range(NX):
        rows = x_ref[yh, core * 4 + s].reshape(NC * JC * ROWS, C)
        q = (dot(rows, wq_ref[...]) * (1.0 / HD**0.5)).astype(BF16)
        q_ref[s] = q.reshape(NC, JC, ROWS, C)
        g_ref[s] = jax.nn.sigmoid(dot(rows, wg_ref[...]) + gs_ref[...]).reshape(NC, JC, ROWS, C)

    project(1 - yh, z // 4)
    project(1 - yh, 1 - z // 4)

    own_head = (
        lax.broadcasted_iota(jnp.int32, (C, C), 0) // HD
        == lax.broadcasted_iota(jnp.int32, (C, C), 1) // HD
    )
    lane_head = lax.broadcasted_iota(jnp.int32, (HD, C), 1) // HD

    def way(dx):
        steps = lax.rem(core * 4 + lax.rem(x + NX - dx, NX) - z + NZ, NZ)
        return jnp.minimum(steps, NZ - steps)

    one, two, three = way(1), way(2), way(3)
    last = jnp.where((one <= two) & (one <= three), 1, jnp.where(three <= two, 3, 2))
    turns = (0, jnp.where(last == 1, 3, 1), jnp.where(last == 2, 3, 2), last)
    for turn, dx in enumerate(turns):
        s = lax.rem(x + NX - dx, NX)
        bias = b_ref.at[s]
        if turn:
            arrived(bias, x_recv.at[dx - 1])
        hidden = []
        for j in range(JC):
            q = q_ref[s, :, j].reshape(NC * ROWS, C)
            q = jnp.where(own_head, jnp.concatenate([q] * H, axis=0), jnp.zeros((), BF16))
            k = k_ref[:, :, :, j].reshape(512, C)
            scores = dot_nt(k, q) + bias[...].reshape(512, C).astype(F32)
            expo = jnp.exp(scores - jnp.max(scores, axis=0, keepdims=True))
            total = jnp.sum(expo, axis=0, keepdims=True)
            expo = expo.astype(BF16)
            acc = jnp.zeros((C, C), F32)
            for p in range(4):
                acc = acc + dot(vt_ref[j, p // 2, p % 2], expo[p * 128 : (p + 1) * 128])
            acc = (acc * (1.0 / total)).T
            att = jnp.zeros((HD, C), F32)
            for h in range(H):
                att = jnp.where(lane_head == h, acc[h * HD : (h + 1) * HD], att)
            hidden.append((g_ref[s, :, j].reshape(NC * ROWS, C) * att).astype(BF16))
        hidden = jnp.stack([v.reshape(NC, ROWS, C) for v in hidden], axis=1)
        update = dot(hidden.reshape(NC * JC * ROWS, C), wo_ref[...]).astype(BF16)
        upd_ref[s] = update.reshape(NC, JC, ROWS, C)
        z_d = core * 4 + s
        for c_d in range(NC):
            mine = (z_d == z) & (core == c_d)
            src, dst = upd_ref.at[s, c_d], out_ref.at[z]
            pl.when(mine)(lambda: pltpu.make_async_copy(src, dst, o_recv).start())
            unless(mine, remote(src, dst, o_send, o_recv, device(c_d, z_d, yh, x, yl)).start)

    arrived(out_ref, o_recv)
    pieces = x_ref.reshape(NZ * 2 * NC, JC, ROWS, C)
    tiles = b_ref.reshape(NX * 32, ROWS, C)
    arrived(pieces.at[pl.ds(0, 7)], n_send)
    arrived(pieces.at[pl.ds(0, 8)], y_send)
    arrived(pieces.at[pl.ds(0, 16)], c_send)
    arrived(b_ref.at[pl.ds(0, 3)], x_send)
    pl.when(out_self)(lambda: arrived(pieces.at[pl.ds(0, 7)], o_send))
    unless(out_self, lambda: arrived(pieces.at[pl.ds(0, 8)], o_send))
    arrived(tiles.at[pl.ds(0, 28)], b_send)
    pl.when(bias_self)(lambda: arrived(tiles.at[pl.ds(0, 3)], t_send))
    unless(bias_self, lambda: arrived(tiles.at[pl.ds(0, 4)], t_send))


def per_device(
    pair_rep, norm_gain, norm_shift, w_query, w_key, w_value, w_bias, w_gate, gate_shift, w_out
):
    dma = pltpu.SemaphoreType.DMA
    result = pl.pallas_call(
        kernel,
        out_shape=jax.ShapeDtypeStruct((NZ, JC, ROWS, C), BF16),
        in_specs=[pl.BlockSpec(memory_space=pltpu.HBM)] * 10,
        out_specs=pl.BlockSpec(memory_space=pltpu.VMEM),
        scratch_shapes=[
            pltpu.VMEM((ROWS, COLS, C), BF16),
            pltpu.VMEM((1, C), F32),
            pltpu.VMEM((1, C), F32),
            pltpu.VMEM((C, C), BF16),
            pltpu.VMEM((C, C), BF16),
            pltpu.VMEM((C, C), BF16),
            pltpu.VMEM((H, C), BF16),
            pltpu.VMEM((C, C), BF16),
            pltpu.VMEM((1, C), F32),
            pltpu.VMEM((C, C), BF16),
            pltpu.VMEM((ROWS * COLS, C), F32),
            pltpu.VMEM((ROWS, C), F32),
            pltpu.VMEM((NZ, JC, ROWS, C), BF16),
            pltpu.VMEM((2, NZ, NC, JC, ROWS, C), BF16),
            pltpu.VMEM((ROWS, C), BF16),
            pltpu.VMEM((NX, 2, NZ, NC, ROWS, C), BF16),
            pltpu.VMEM((2, NZ, NC, JC, ROWS, C), BF16),
            pltpu.VMEM((JC, 2, 2, C, 8 * ROWS), BF16),
            pltpu.VMEM((NX, NC, JC, ROWS, C), BF16),
            pltpu.VMEM((NX, NC, JC, ROWS, C), F32),
            pltpu.VMEM((NX, NC, JC, ROWS, C), BF16),
            dma((9,)), dma((4,)),
            dma, dma, dma, dma((NZ,)), dma, dma((NZ,)), dma, dma, dma((NZ,)),
            dma, dma((NZ,)), dma, dma((NX - 1,)), dma, dma,
        ],
        compiler_params=pltpu.CompilerParams(
            collective_id=0, has_side_effects=True, vmem_limit_bytes=32 << 20
        ),
        name="triangle",
    )(*(
        pltpu.with_memory_space_constraint(v, pltpu.HBM)
        for v in (
            pair_rep, norm_gain.reshape(1, C), norm_shift.reshape(1, C), w_query, w_key, w_value,
            w_bias.T, w_gate, gate_shift.reshape(1, C), w_out,
        )
    ))
    return result.reshape(COLS, ROWS, C).transpose(1, 0, 2)


def solution(mesh):
    placed = (P("blk", "col", None),) + (P(),) * 9
    return jax.shard_map(
        per_device, mesh=mesh, in_specs=placed, out_specs=P("blk", "col", None), check_vma=False
    )
```

```python
import jax
import jax.numpy as jnp
from jax import lax
from jax.experimental import pallas as pl
from jax.experimental.pallas import tpu as pltpu
from jax.sharding import PartitionSpec as P

MESH = pl.DeviceIdType.MESH
ROWS, COLS, C, H, HD = 16, 32, 128, 4, 32
NZ, NX, NY, NC = 8, 4, 4, 2
FAR = (4, 3, 5, 2, 6, 1, 7, 0)
NEAR = (0, 1, 7, 2, 6, 3, 5, 4)
JC = 4
F32, BF16 = jnp.float32, jnp.bfloat16


def device(core, z, yh, x, yl):
    return ((yh * NZ + z) * NC + core, yl * NX + x)


def remote(src, dst, send, recv, where):
    return pltpu.make_async_remote_copy(
        src_ref=src, dst_ref=dst, send_sem=send, recv_sem=recv, device_id=where, device_id_type=MESH
    )


def dot(a, b):
    return jnp.dot(a, b, preferred_element_type=F32)


def dot_nt(a, b):
    return lax.dot_general(a, b, (((1,), (1,)), ((), ())), preferred_element_type=F32)


def kernel(
    pair_hbm, gain_hbm, shift_hbm, wq_hbm, wk_hbm, wv_hbm, wb_hbm, wg_hbm, gs_hbm, wo_hbm,
    out_ref,
    pair_ref, gain_ref, shift_ref, wq_ref, wk_ref, wv_ref, wb_ref, wg_ref, gs_ref, wo_ref,
    ln_ref, norm_ref, part_ref, x_ref, tile_ref, b_ref, k_ref, vt_ref, q_ref, g_ref, upd_ref,
    in_sem, pair_sem,
    t_send, t_recv, n_send, n_recv, y_send, y_recv, c_send, h_recv, c_recv, b_send, b_recv, x_send, x_recv, o_send, o_recv,
):
    loads = []
    for r in range(4):
        rows = pl.ds(r * 4, 4)
        loads.append(pltpu.make_async_copy(pair_hbm.at[rows], pair_ref.at[rows], pair_sem.at[r]))
    for i, (src, dst) in enumerate((
        (gain_hbm, gain_ref), (shift_hbm, shift_ref), (wb_hbm, wb_ref), (wk_hbm, wk_ref),
        (wv_hbm, wv_ref), (wq_hbm, wq_ref), (wg_hbm, wg_ref), (gs_hbm, gs_ref), (wo_hbm, wo_ref),
    )):
        loads.append(pltpu.make_async_copy(src, dst, in_sem.at[i]))
    for cp in loads[:7]:
        cp.start()
    blk, col = lax.axis_index("blk"), lax.axis_index("col")
    core, z, yh = lax.rem(blk, NC), lax.rem(blk // NC, NZ), blk // (NC * NZ)
    x, yl = lax.rem(col, NX), col // NX
    other = 1 - core
    bias_yl = yh * NC + core
    to_yh, to_core = yl // NC, lax.rem(yl, NC)
    bias_self = bias_yl == yl
    out_self = core == z // 4

    barrier = pltpu.get_barrier_semaphore()

    def greet(where):
        pl.semaphore_signal(barrier, inc=1, device_id=where, device_id_type=MESH)

    def unless(condition, action):
        pl.when(jnp.logical_not(condition))(action)

    for dz in FAR:
        z_s = lax.rem(z + dz, NZ)
        if dz:
            greet(device(core, z_s, yh, x, yl))
        unless(out_self & (dz == 0), lambda: greet(device(z // 4, z_s, yh, x, yl)))
    for yh_s in range(2):
        for c_s in range(NC):
            mine = bias_self & (c_s == core) & (yh_s == yh)
            unless(mine, lambda: greet(device(c_s, z, yh_s, x, bias_yl)))
    greet(device(core, z, 1 - yh, x, yl))
    for dx in range(1, NX):
        greet(device(core, z, yh, lax.rem(x + dx, NX), yl))
    greet(device(other, z, yh, x, yl))


    for cp in loads[4:7]:
        cp.wait()
    wide = jnp.concatenate([jnp.broadcast_to(wb_ref[h : h + 1].astype(F32), (HD, C)) for h in range(H)])
    wide = wide.astype(BF16)
    diagonal = (
        lax.broadcasted_iota(jnp.int32, (COLS, C), 0)
        == lax.broadcasted_iota(jnp.int32, (COLS, C), 1) % HD
    )
    gain, shift = gain_ref[...], shift_ref[...]
    for r in range(0, ROWS, 16):
        for cp in loads[r // 4 : (r + 16) // 4]:
            cp.wait()
        v = pair_ref[r : r + 16].reshape(16 * COLS, C).astype(F32)
        v = v - jnp.mean(v, axis=-1, keepdims=True)
        var = jnp.mean(v * v, axis=-1, keepdims=True)
        n = (v * lax.rsqrt(var + 1e-05) * gain + shift).astype(BF16)
        ln_ref[r * COLS : (r + 16) * COLS, :] = n.astype(F32)
        t = dot_nt(n, wide).reshape(16, COLS, C)
        norm_ref[r : r + 16, :] = jnp.sum(jnp.where(diagonal[None], t, 0.0), axis=1)
    tile_ref[...] = norm_ref[...].astype(BF16)

    for j in range(COLS):
        part_ref[j // JC, j % JC] = ln_ref[pl.ds(j, ROWS, stride=COLS), :].astype(BF16)

    sends_bias = 4 - bias_self.astype(jnp.int32)
    sends_out = 8 - out_self.astype(jnp.int32)
    pl.semaphore_wait(barrier, sends_bias + sends_out + 12)

    for dz in FAR:
        z_d = lax.rem(z + dz, NZ)
        if dz:
            remote(
                part_ref.at[z_d], x_ref.at[yh, z, core], n_send, n_recv.at[z],
                device(core, z_d, yh, x, yl),
            ).start()
        else:
            pltpu.make_async_copy(part_ref.at[z], x_ref.at[yh, z, core], n_recv.at[z]).start()

    for cp in loads[7:]:
        cp.start()

    tile_dst = b_ref.at[x, yh, z, core]
    for dy in (2, 1, 3, 0):
        yl_d = lax.rem(yl + dy, NY)
        cp = remote(tile_ref, tile_dst, t_send, t_recv, device(to_core, z, to_yh, x, yl_d))
        if dy:
            cp.start()
        else:
            pl.when(bias_self)(lambda: pltpu.make_async_copy(tile_ref, tile_dst, t_recv).start())
            unless(bias_self, cp.start)

    def arrived(ref, sem):
        pltpu.make_async_copy(ref, ref, sem).wait()

    def share(dz):
        z_s = lax.rem(z + dz, NZ)
        here = x_ref.at[yh, z_s, core]
        arrived(here, n_recv.at[z_s])
        remote(here, here, y_send, y_recv.at[z_s], device(core, z, 1 - yh, x, yl)).start()

    def spread(dz):
        z_s = lax.rem(z + dz, NZ)
        got = b_ref.at[x, :, z_s]
        if dz:
            arrived(got, b_recv.at[z_s])
        for dx in (2, 1, 3):
            remote(
                got, got, x_send, x_recv.at[dx - 1], device(core, z, yh, lax.rem(x + dx, NX), yl)
            ).start()

    def share_other():
        for dz in NEAR:
            z_s = lax.rem(z + dz, NZ)
            there = x_ref.at[1 - yh, z_s, core]
            arrived(there, y_recv.at[z_s])
            remote(there, there, c_send, c_recv.at[z_s], device(other, z, yh, x, yl)).start()

    share(0)
    own_z = b_ref.at[x, :, z]
    arrived(own_z, t_recv)
    for dz in FAR[:-1]:
        remote(
            own_z, own_z, b_send, b_recv.at[z], device(core, lax.rem(z + dz, NZ), yh, x, yl)
        ).start()
    spread(0)
    for dz in NEAR[1:]:
        share(dz)
    mine = x_ref.at[yh, :, core]
    remote(mine, mine, c_send, h_recv, device(other, z, yh, x, yl)).start()
    for dz in NEAR[1:]:
        spread(dz)

    for cp in loads[7:]:
        cp.wait()
    wk = wk_ref[...]
    wvt = wv_ref[...].astype(F32).T.astype(BF16)

    def project(half, four):
        if half is not yh:
            for z_s in range(4):
                z_s = four * 4 + z_s
                arrived(x_ref.at[half, z_s, other], c_recv.at[z_s])
        part = x_ref.at[half, pl.ds(four * 4, 4)]
        rows = part[...].reshape(8 * JC * ROWS, C)
        k_ref[half, pl.ds(four * 4, 4)] = dot(rows, wk).astype(BF16).reshape(4, NC, JC, ROWS, C)
        for j in range(JC):
            vt_ref[j, half, four] = dot_nt(wvt, part[:, :, j].reshape(8 * ROWS, C)).astype(BF16)

    arrived(x_ref.at[yh, :, other], h_recv)
    project(yh, z // 4)
    project(yh, 1 - z // 4)
    own_head = (
        lax.broadcasted_iota(jnp.int32, (C, C), 0) // HD
        == lax.broadcasted_iota(jnp.int32, (C, C), 1) // HD
    )
    wqt = wq_ref[...].astype(F32).T.astype(BF16)
    for s in range(NX):
        block = x_ref.at[yh, core * 4 + s]
        for j in range(JC):
            rows = block[:, j].reshape(NC * ROWS, C)
            q = dot_nt(wqt, jnp.concatenate([rows] * H, axis=0)) * (1.0 / HD**0.5)
            q_ref[s, j] = jnp.where(own_head, q, 0.0).astype(BF16)
        gate = jax.nn.sigmoid(dot(block[...].reshape(NC * JC * ROWS, C), wg_ref[...]) + gs_ref[...])
        g_ref[s] = gate.reshape(NC, JC, ROWS, C)

    share_other()

    project(1 - yh, z // 4)
    project(1 - yh, 1 - z // 4)

    lane_head = lax.broadcasted_iota(jnp.int32, (HD, C), 1) // HD

    def way(dx):
        steps = lax.rem(core * 4 + lax.rem(x + NX - dx, NX) - z + NZ, NZ)
        return jnp.minimum(steps, NZ - steps)

    one, two, three = way(1), way(2), way(3)
    last = jnp.where((one <= two) & (one <= three), 1, jnp.where(three <= two, 3, 2))
    turns = (0, jnp.where(last == 1, 3, 1), jnp.where(last == 2, 3, 2), last)
    for turn, dx in enumerate(turns):
        s = lax.rem(x + NX - dx, NX)
        bias = b_ref.at[s]
        if turn:
            arrived(bias, x_recv.at[dx - 1])
        hidden = []
        for j in range(JC):
            k = k_ref[:, :, :, j].reshape(512, C)
            scores = dot(k, q_ref[s, j]) + bias[...].reshape(512, C).astype(F32)
            expo = jnp.exp(scores - jnp.max(scores, axis=0, keepdims=True))
            total = jnp.sum(expo, axis=0, keepdims=True)
            expo = expo.astype(BF16)
            acc = jnp.zeros((C, C), F32)
            for p in range(4):
                acc = acc + dot(vt_ref[j, p // 2, p % 2], expo[p * 128 : (p + 1) * 128])
            acc = (acc * (1.0 / total)).T
            att = jnp.zeros((HD, C), F32)
            for h in range(H):
                att = jnp.where(lane_head == h, acc[h * HD : (h + 1) * HD], att)
            hidden.append((g_ref[s, :, j].reshape(NC * ROWS, C) * att).astype(BF16))
        hidden = jnp.stack([v.reshape(NC, ROWS, C) for v in hidden], axis=1)
        update = dot(hidden.reshape(NC * JC * ROWS, C), wo_ref[...]).astype(BF16)
        upd_ref[s] = update.reshape(NC, JC, ROWS, C)
        z_d = core * 4 + s
        for c_d in range(NC):
            mine = (z_d == z) & (core == c_d)
            src, dst = upd_ref.at[s, c_d], out_ref.at[z]
            pl.when(mine)(lambda: pltpu.make_async_copy(src, dst, o_recv).start())
            unless(mine, remote(src, dst, o_send, o_recv, device(c_d, z_d, yh, x, yl)).start)

    arrived(out_ref, o_recv)
    pieces = x_ref.reshape(NZ * 2 * NC, JC, ROWS, C)
    tiles = b_ref.reshape(NX * 32, ROWS, C)
    arrived(pieces.at[pl.ds(0, 7)], n_send)
    arrived(pieces.at[pl.ds(0, 8)], y_send)
    arrived(pieces.at[pl.ds(0, 16)], c_send)
    arrived(b_ref.at[pl.ds(0, 3)], x_send)
    pl.when(out_self)(lambda: arrived(pieces.at[pl.ds(0, 7)], o_send))
    unless(out_self, lambda: arrived(pieces.at[pl.ds(0, 8)], o_send))
    arrived(tiles.at[pl.ds(0, 28)], b_send)
    pl.when(bias_self)(lambda: arrived(tiles.at[pl.ds(0, 3)], t_send))
    unless(bias_self, lambda: arrived(tiles.at[pl.ds(0, 4)], t_send))


def per_device(
    pair_rep, norm_gain, norm_shift, w_query, w_key, w_value, w_bias, w_gate, gate_shift, w_out
):
    dma = pltpu.SemaphoreType.DMA
    result = pl.pallas_call(
        kernel,
        out_shape=jax.ShapeDtypeStruct((NZ, JC, ROWS, C), BF16),
        in_specs=[pl.BlockSpec(memory_space=pltpu.HBM)] * 10,
        out_specs=pl.BlockSpec(memory_space=pltpu.VMEM),
        scratch_shapes=[
            pltpu.VMEM((ROWS, COLS, C), BF16),
            pltpu.VMEM((1, C), F32),
            pltpu.VMEM((1, C), F32),
            pltpu.VMEM((C, C), BF16),
            pltpu.VMEM((C, C), BF16),
            pltpu.VMEM((C, C), BF16),
            pltpu.VMEM((H, C), BF16),
            pltpu.VMEM((C, C), BF16),
            pltpu.VMEM((1, C), F32),
            pltpu.VMEM((C, C), BF16),
            pltpu.VMEM((ROWS * COLS, C), F32),
            pltpu.VMEM((ROWS, C), F32),
            pltpu.VMEM((NZ, JC, ROWS, C), BF16),
            pltpu.VMEM((2, NZ, NC, JC, ROWS, C), BF16),
            pltpu.VMEM((ROWS, C), BF16),
            pltpu.VMEM((NX, 2, NZ, NC, ROWS, C), BF16),
            pltpu.VMEM((2, NZ, NC, JC, ROWS, C), BF16),
            pltpu.VMEM((JC, 2, 2, C, 8 * ROWS), BF16),
            pltpu.VMEM((NX, JC, C, C), BF16),
            pltpu.VMEM((NX, NC, JC, ROWS, C), F32),
            pltpu.VMEM((NX, NC, JC, ROWS, C), BF16),
            dma((9,)), dma((4,)),
            dma, dma, dma, dma((NZ,)), dma, dma((NZ,)), dma, dma, dma((NZ,)),
            dma, dma((NZ,)), dma, dma((NX - 1,)), dma, dma,
        ],
        compiler_params=pltpu.CompilerParams(
            collective_id=0, has_side_effects=True, vmem_limit_bytes=32 << 20
        ),
        name="triangle",
    )(*(
        pltpu.with_memory_space_constraint(v, pltpu.HBM)
        for v in (
            pair_rep, norm_gain.reshape(1, C), norm_shift.reshape(1, C), w_query, w_key, w_value,
            w_bias.T, w_gate, gate_shift.reshape(1, C), w_out,
        )
    ))
    return result.reshape(COLS, ROWS, C).transpose(1, 0, 2)


def solution(mesh):
    placed = (P("blk", "col", None),) + (P(),) * 9
    return jax.shard_map(
        per_device, mesh=mesh, in_specs=placed, out_specs=P("blk", "col", None), check_vma=False
    )
```
